512 devices in a mesh: mirror: 32 (over y, z_hi, core), blk: 16 (over x, z_lo).
Axes of the slice: x: 4, y: 8, z: 8 (z_hi: 2, z_lo: 4; z = z_hi * 4 + z_lo), core: 2. Of those that a mesh axis runs over, the one named last changes fastest.
Arguments:
- colloc: float32 [4096, 2048], P('blk'), may hold values from -2 to 2
- coeffs: float32 [128, 4096], P('blk'), may hold values from -6 to 6
- targets: float32 [32, 128, 128, 128], P('mirror', 'blk'), may hold values from -6 to 6
- pair_list: int32 [32, 2], P('mirror'), may hold values from 0 to 15, as said below
Outputs:
- residual: float32 [32, 128, 128, 128], P('mirror', 'blk')
- gradient: float32 [128, 4096], P('blk', 'mirror')
The draws below stay inside these ranges and needn't reach their ends.
Inputs may be any that keep to these rules, and one draw needn't show every extreme that they name: `pair_list`: p != q in every row, and for m < 16 row m + 16 holds the row m reversed, (q, p).
All inputs are finite; a program needn't handle non-finite values.
Results may differ from the reference program's by a relative error of at most 0.0003.
Values sent between devices are 32-bit elements; how exact they have to be, the bound alone decides.
No kernel may reach another device: no remote copies, remote signals or barrier semaphores. Data moves between devices by JAX's collectives and lax.ppermute only.
A program may use at most 64 MiB of HBM per device.

```python
import jax
import jax.numpy as jnp
from jax import lax

NORB = 2048
NB = 128
G = 4096
AUX = 128
SB = 32


def draw_pair_list(key, part):
    key = jax.random.fold_in(key, 7)
    first_key, second_key = jax.random.split(key)
    half_count = SB // 2
    block_total = NORB // NB
    left_ids = jax.random.randint(first_key, (half_count,), 0, block_total)
    offsets = jax.random.randint(second_key, (half_count,), 1, block_total)
    left_ids = left_ids.at[0].set(block_total - 1)
    offsets = offsets.at[0].set(1)
    right_ids = (left_ids + offsets) % block_total
    front = jnp.stack([left_ids, right_ids], axis=1)
    back = jnp.stack([right_ids, left_ids], axis=1)
    return jnp.concatenate([front, back], axis=0).astype(jnp.int32)


def levels(rng, extent, cuts, least, largest):
    loudness = 1.0
    for dim, parts in cuts:
        draws = jax.random.uniform(jax.random.fold_in(jax.random.fold_in(rng, 6), dim), (parts,), jnp.float32, least / len(cuts), largest / len(cuts))
        loudness = loudness * jnp.repeat(jnp.exp(draws), extent[dim] // parts).reshape((-1,) + (1,) * (len(extent) - 1 - dim))
    return loudness


def normal_values(own_key, shape, width, bound, pieces=(), held_as=jnp.bfloat16):
    array = jax.random.normal(own_key, shape, jnp.float32) * width
    if len(pieces) > 0:
        array = levels(own_key, shape, pieces, -0.22, 0.18) * array
    return jnp.clip(array, min=-bound, max=bound).astype(held_as)


def setup_inputs(seed: int = 0) -> dict:
    seeds = jax.random.split(jax.random.key(seed), 5)
    colloc = normal_values(seeds[0], (G, NORB), 0.125, 2.0, ((0, 16),), jnp.float32)
    coeffs = normal_values(seeds[1], (AUX, G), 1.0, 6.0, ((0, 16),), jnp.float32)
    targets = normal_values(seeds[2], (SB, AUX, NB, NB), 1.0, 6.0, ((0, 32), (1, 16)), jnp.float32)
    pair_list = draw_pair_list(jax.random.fold_in(seeds[4], 71), 0)
    return dict(colloc=colloc, coeffs=coeffs, targets=targets, pair_list=pair_list)


highest = lax.Precision.HIGHEST


def reference(colloc, coeffs, targets, pair_list):
    half_count = SB // 2
    partner_ids = ((jnp.arange(SB, dtype=jnp.int32) + half_count) % SB).astype(jnp.int32)
    symmetric = 0.5 * (targets + jnp.swapaxes(targets[partner_ids], 2, 3))

    def one_block(block_index):
        left_start = (pair_list[block_index, 0] * NB).astype(jnp.int32)
        right_start = (pair_list[block_index, 1] * NB).astype(jnp.int32)
        left_cols = lax.dynamic_slice_in_dim(colloc, left_start, NB, 1)
        right_cols = lax.dynamic_slice_in_dim(colloc, right_start, NB, 1)
        weighted = coeffs[:, :, None] * left_cols[None]
        fitted = jnp.einsum('agp,gq->apq', weighted, right_cols, precision=highest)
        residual_block = symmetric[block_index] - fitted
        misfit = targets[block_index] - fitted
        spread = jnp.einsum('gp,apq->agq', left_cols, misfit, precision=highest)
        return residual_block, jnp.sum(spread * right_cols[None], axis=2)

    residual, grid_terms = lax.map(one_block, jnp.arange(SB, dtype=jnp.int32))
    return residual, jnp.sum(grid_terms, axis=0)
```

```python
import jax
import jax.numpy as jnp
from jax import lax
from jax.experimental import pallas as pl
from jax.experimental.pallas import tpu as pltpu
from jax.sharding import PartitionSpec as P

NX, NZ = 4, 4
NY, NZH, NC = 8, 2, 2
MIRROR = NY * NZH * NC
HALF = MIRROR // 2
bf16, f32 = jnp.bfloat16, jnp.float32
VMEM = pl.BlockSpec(memory_space=pltpu.VMEM)
SMEM = pl.BlockSpec(memory_space=pltpu.SMEM)
ANY = pl.BlockSpec(memory_space=pl.ANY)


def params(mib=32):
    return pltpu.CompilerParams(vmem_limit_bytes=mib * 1024 * 1024)


def swap_pairs():
    out = []
    for m in range(MIRROR):
        low = m < HALF
        if low and m % 2 == 1:
            out.append((m, m + HALF - 1))
        elif not low and m % 2 == 0:
            out.append((m, m - HALF + 1))
        else:
            out.append((m, m))
    return out


def x_shift(by):
    return [(x * NZ + z, ((x + by) % NX) * NZ + z) for x in range(NX) for z in range(NZ)]


def split(v):
    hi = v.astype(bf16)
    return hi, (v - hi.astype(f32)).astype(bf16)


def pick_kernel(mine_ref, mate_ref, colloc_ref, out_ref, sems):
    m = lax.axis_index("mirror")
    core = lax.rem(m, 2)
    low = (m < HALF).astype(jnp.int32)
    keeps = core != low
    p = jnp.where(keeps, mine_ref[0, 0], mate_ref[0, 1])
    q = jnp.where(keeps, mine_ref[0, 1], mate_ref[0, 0])
    n = out_ref.shape[0]
    row = pl.multiple_of(core * n, n)
    copies = []
    for k, block in enumerate((p, q)):
        copies.append(
            pltpu.make_async_copy(
                colloc_ref.at[pl.ds(row, n), pl.ds(pl.multiple_of(block * 128, 128), 128)],
                out_ref.at[:, pl.ds(k * 128, 128)],
                sems.at[k],
            )
        )
    for c in copies:
        c.start()
    for c in copies:
        c.wait()


def fit_kernel(own_ref, below_ref, above_ref, opp0_ref, opp1_ref, coef_ref, t_ref, u_ref, lt_ref, rt_ref, whi, wlo, acc):
    core = lax.rem(lax.axis_index("mirror"), 2)
    x = lax.axis_index("blk") // NZ
    naux = coef_ref.shape[0]
    sources = (
        (0, (own_ref,)),
        (NX - 1, (below_ref,)),
        (1, (above_ref,)),
        (2, (opp0_ref, opp1_ref)),
    )
    for n, (dx, refs) in enumerate(sources):
        xs = lax.rem(x + dx, NX)
        rows = jnp.concatenate([r[...] for r in refs], axis=0) if len(refs) > 1 else refs[0][...]
        left, right = rows[:, :128], rows[:, 128:]
        lt, rt = left.T, right.T
        lt_ref[:, pl.ds(n * 512, 512)] = lt
        rhi, rlo = split(right)
        rthi, rtlo = split(rt)
        rt_ref[0:128, pl.ds(n * 512, 512)] = rthi
        rt_ref[128:256, pl.ds(n * 512, 512)] = rtlo
        both = jnp.concatenate([rhi, rlo], axis=1)
        cs = []
        for z in range(NZ):
            at = pl.multiple_of((xs * NZ + z) * 256 + core * 128, 128)
            cs.append(coef_ref[:, pl.ds(at, 128)])
        cf = jnp.concatenate(cs, axis=1)
        for a in range(naux):
            hi, lo = split(cf[a : a + 1, :] * lt)
            whi[pl.ds(a * 128, 128), :] = hi
            wlo[pl.ds(a * 128, 128), :] = lo
        part = jnp.dot(whi[...], both, preferred_element_type=f32)
        part += jnp.dot(wlo[...], both, preferred_element_type=f32)
        if n == 0:
            acc[...] = part
        elif n < len(sources) - 1:
            acc[...] += part
        else:
            tot = acc[...] + part
            fit = tot[:, :128] + tot[:, 128:]
            u_ref[...] = 0.5 * t_ref[...] - fit.reshape(naux, 128, 128)


def residual_kernel(u_ref, o_ref, r_ref):
    for a in range(u_ref.shape[0]):
        r_ref[a] = u_ref[a] + o_ref[a].T


def gradient_kernel(r_ref, lt_ref, rt_ref, keep_ref, send_ref, hh, ll, parts):
    m = lax.axis_index("mirror")
    zh = lax.rem(m // NC, NZH)
    x = lax.axis_index("blk") // NZ
    naux = r_ref.shape[0]
    for a in range(naux):
        hi, lo = split(2.0 * r_ref[a])
        hh[pl.ds(a * 128, 128), 0:128] = hi
        hh[pl.ds(a * 128, 128), 128:256] = hi
        ll[pl.ds(a * 128, 128), 0:128] = lo
        ll[pl.ds(a * 128, 128), 128:256] = lo
    for n, dx in enumerate((0, NX - 1, 1, 2)):
        xs = lax.rem(x + dx, NX)
        for h in range(2):
            cols = pl.ds(n * 512 + h * 256, 256)
            rt = rt_ref[:, cols]
            spread = jnp.dot(hh[...], rt, preferred_element_type=f32)
            spread += jnp.dot(ll[...], rt, preferred_element_type=f32)
            lt = lt_ref[:, cols]
            terms = []
            for a in range(naux):
                terms.append(jnp.sum(spread[a * 128 : (a + 1) * 128] * lt, axis=0, keepdims=True))
            block = jnp.concatenate(terms, axis=0)
            for z in range(2):
                parts[xs * NZ + h * 2 + z] = block[:, z * 128 : (z + 1) * 128]
    for y in range(NY):
        keep_ref[y] = parts[y * NZH + zh]
        send_ref[y] = parts[y * NZH + 1 - zh]


def per_device(colloc, coeffs, targets, pair_list):
    naux, nb = targets.shape[1], targets.shape[2]
    mate = lax.ppermute(pair_list, "mirror", [(m, m ^ 1) for m in range(MIRROR)])
    work = lax.ppermute(targets, "mirror", swap_pairs())[0]

    rows = pl.pallas_call(
        pick_kernel,
        out_shape=jax.ShapeDtypeStruct((colloc.shape[0] // 2, 2 * nb), f32),
        in_specs=[SMEM, SMEM, ANY],
        out_specs=VMEM,
        scratch_shapes=[pltpu.SemaphoreType.DMA((2,))],
        compiler_params=params(8),
        name="pick",
    )(pair_list, mate, colloc)

    z_groups = [[x * NZ + z for z in range(NZ)] for x in range(NX)]
    own = lax.all_gather(rows, "blk", axis=0, tiled=True, axis_index_groups=z_groups)
    below = lax.ppermute(own, "blk", x_shift(1))
    above = lax.ppermute(own, "blk", x_shift(-1))
    h = own.shape[0] // 2
    opp0 = lax.ppermute(below[:h], "blk", x_shift(1))
    opp1 = lax.ppermute(above[h:], "blk", x_shift(-1))

    u, lt, rt = pl.pallas_call(
        fit_kernel,
        out_shape=(
            jax.ShapeDtypeStruct((naux, nb, nb), f32),
            jax.ShapeDtypeStruct((nb, 2048), f32),
            jax.ShapeDtypeStruct((2 * nb, 2048), bf16),
        ),
        in_specs=[VMEM] * 7,
        out_specs=[VMEM] * 3,
        scratch_shapes=[
            pltpu.VMEM((naux * nb, 512), bf16),
            pltpu.VMEM((naux * nb, 512), bf16),
            pltpu.VMEM((naux * nb, 2 * nb), f32),
        ],
        compiler_params=params(),
        cost_estimate=pl.CostEstimate(flops=4 * 2 * 1024 * 2048 * 128, bytes_accessed=6 << 20, transcendentals=0),
        name="fit",
    )(own, below, above, opp0, opp1, coeffs, work)

    other = lax.ppermute(u, "mirror", [(m, m ^ 1) for m in range(MIRROR)])
    res = pl.pallas_call(
        residual_kernel,
        out_shape=jax.ShapeDtypeStruct((naux, nb, nb), f32),
        in_specs=[VMEM] * 2,
        out_specs=VMEM,
        compiler_params=params(16),
        cost_estimate=pl.CostEstimate(flops=1 << 17, bytes_accessed=3 << 19, transcendentals=0),
        name="residual",
    )(u, other)
    residual = lax.ppermute(res[None], "mirror", swap_pairs())

    keep, send = pl.pallas_call(
        gradient_kernel,
        out_shape=(jax.ShapeDtypeStruct((NY, naux, nb), f32),) * 2,
        in_specs=[VMEM] * 3,
        out_specs=[VMEM] * 2,
        scratch_shapes=[
            pltpu.VMEM((naux * nb, 2 * nb), bf16),
            pltpu.VMEM((naux * nb, 2 * nb), bf16),
            pltpu.VMEM((NX * NZ, naux, nb), f32),
        ],
        compiler_params=params(),
        cost_estimate=pl.CostEstimate(flops=4 * 2 * 1024 * 2048 * 128, bytes_accessed=4 << 20, transcendentals=0),
        name="gradient",
    )(res, lt, rt)
    flip = [(m, m ^ NC) for m in range(MIRROR)]
    half_sum = keep + lax.ppermute(send, "mirror", flip)
    y_groups = [[(y * NZH + h) * NC + c for y in range(NY)] for h in range(NZH) for c in range(NC)]
    spread = lax.all_to_all(half_sum, "mirror", 0, 0, tiled=True, axis_index_groups=y_groups)
    return residual, jnp.sum(spread, axis=0)


def solution(mesh):
    return jax.shard_map(
        per_device,
        mesh=mesh,
        in_specs=(
            P("blk", None),
            P("blk", None),
            P("mirror", "blk", None, None),
            P("mirror", None),
        ),
        out_specs=(P("mirror", "blk", None, None), P("blk", "mirror")),
        check_vma=False,
    )
```

```python
import jax
import jax.numpy as jnp
from jax import lax
from jax.experimental import pallas as pl
from jax.experimental.pallas import tpu as pltpu
from jax.sharding import PartitionSpec as P

NX, NZ = 4, 4
NY, NZH, NC = 8, 2, 2
MIRROR = NY * NZH * NC
HALF = MIRROR // 2
bf16, f32 = jnp.bfloat16, jnp.float32
VMEM = pl.BlockSpec(memory_space=pltpu.VMEM)
SMEM = pl.BlockSpec(memory_space=pltpu.SMEM)
ANY = pl.BlockSpec(memory_space=pl.ANY)


def params(mib):
    return pltpu.CompilerParams(vmem_limit_bytes=mib * 1024 * 1024)


def cost(flops, mib):
    return pl.CostEstimate(flops=flops, bytes_accessed=mib << 20, transcendentals=0)


def swap_pairs():
    out = []
    for m in range(MIRROR):
        low = m < HALF
        if low and m % 2 == 1:
            out.append((m, m + HALF - 1))
        elif not low and m % 2 == 0:
            out.append((m, m - HALF + 1))
        else:
            out.append((m, m))
    return out


def x_trade(mask):
    return [(x * NZ + z, (x ^ mask) * NZ + z) for x in range(NX) for z in range(NZ)]


def sources(x):
    return [x, x + 1 - 2 * lax.rem(x, 2), NX - 1 - x, lax.rem(x + 2, NX)]


def split(v):
    hi = v.astype(bf16)
    return hi, (v - hi.astype(f32)).astype(bf16)


def pick_kernel(mine_ref, mate_ref, colloc_ref, out_ref, sems):
    m = lax.axis_index("mirror")
    core = lax.rem(m, 2)
    keeps = core != (m < HALF).astype(jnp.int32)
    p = jnp.where(keeps, mine_ref[0, 0], mate_ref[0, 1])
    q = jnp.where(keeps, mine_ref[0, 1], mate_ref[0, 0])
    n = out_ref.shape[0]
    row = pl.multiple_of(core * n, n)
    copies = []
    for k, block in enumerate((p, q)):
        copies.append(
            pltpu.make_async_copy(
                colloc_ref.at[pl.ds(row, n), pl.ds(pl.multiple_of(block * 128, 128), 128)],
                out_ref.at[:, pl.ds(k * 128, 128)],
                sems.at[k],
            )
        )
    for c in copies:
        c.start()
    for c in copies:
        c.wait()


def fit_part(coef_ref, rows, xs, lt_ref, rt_ref, n, whi, wlo):
    core = lax.rem(lax.axis_index("mirror"), 2)
    left, right = rows[:, :128], rows[:, 128:]
    lt, rt = left.T, right.T
    cols = pl.ds(n * 512, 512)
    lt_ref[:, cols] = lt
    rhi, rlo = split(right)
    rthi, rtlo = split(rt)
    rt_ref[0:128, cols] = rthi
    rt_ref[128:256, cols] = rtlo
    both = jnp.concatenate([rhi, rlo], axis=1)
    cs = []
    for z in range(NZ):
        at = pl.multiple_of((xs * NZ + z) * 256 + core * 128, 128)
        cs.append(coef_ref[:, pl.ds(at, 128)])
    cf = jnp.concatenate(cs, axis=1)
    for a in range(coef_ref.shape[0]):
        hi, lo = split(cf[a : a + 1, :] * lt)
        whi[pl.ds(a * 128, 128), :] = hi
        wlo[pl.ds(a * 128, 128), :] = lo
    part = jnp.dot(whi[...], both, preferred_element_type=f32)
    return part + jnp.dot(wlo[...], both, preferred_element_type=f32)


def fit_first_kernel(own, near0, near1, side0, side1, coef_ref, acc_ref, lt_ref, rt_ref, whi, wlo):
    xs = sources(lax.axis_index("blk") // NZ)
    for n, refs in enumerate(((own,), (near0, near1), (side0, side1))):
        rows = jnp.concatenate([r[...] for r in refs], axis=0)
        part = fit_part(coef_ref, rows, xs[n], lt_ref, rt_ref, n, whi, wlo)
        if n == 0:
            acc_ref[...] = part
        else:
            acc_ref[...] += part


def fit_last_kernel(far0, far1, acc_ref, coef_ref, t_ref, u_ref, lt_ref, rt_ref, whi, wlo):
    xs = sources(lax.axis_index("blk") // NZ)
    rows = jnp.concatenate([far0[...], far1[...]], axis=0)
    tot = acc_ref[...] + fit_part(coef_ref, rows, xs[3], lt_ref, rt_ref, 0, whi, wlo)
    fit = tot[:, :128] + tot[:, 128:]
    u_ref[...] = 0.5 * t_ref[...] - fit.reshape(t_ref.shape)


def blocks(parity, lt_refs, rt_refs, out_ref, hh, ll):
    for n, xs in enumerate(sources(lax.axis_index("blk") // NZ)):
        lt_ref, rt_ref = (lt_refs[0], rt_refs[0]) if n < 3 else (lt_refs[1], rt_refs[1])
        at = n * 512 if n < 3 else 0
        cols = [pl.ds(pl.multiple_of(at + j * 256 + parity * 128, 128), 128) for j in range(2)]
        rt = jnp.concatenate([rt_ref[:, c] for c in cols], axis=1)
        lt = jnp.concatenate([lt_ref[:, c] for c in cols], axis=1)
        spread = jnp.dot(hh[...], rt, preferred_element_type=f32)
        spread += jnp.dot(ll[...], rt, preferred_element_type=f32)
        terms = []
        for a in range(out_ref.shape[1]):
            terms.append(jnp.sum(spread[a * 128 : (a + 1) * 128] * lt, axis=0, keepdims=True))
        block = jnp.concatenate(terms, axis=0)
        for j in range(2):
            out_ref[xs * 2 + j] = block[:, j * 128 : (j + 1) * 128]


def send_kernel(u_ref, o_ref, lt0, lt1, rt0, rt1, out_ref, hh_ref, ll_ref, r_ref):
    zh = lax.rem(lax.axis_index("mirror") // NC, NZH)
    for a in range(u_ref.shape[0]):
        r = u_ref[a] + o_ref[a].T
        r_ref[a] = r
        hi, lo = split(2.0 * r)
        rows = pl.ds(a * 128, 128)
        hh_ref[rows, 0:128] = hi
        hh_ref[rows, 128:256] = hi
        ll_ref[rows, 0:128] = lo
        ll_ref[rows, 128:256] = lo
    blocks(1 - zh, (lt0, lt1), (rt0, rt1), out_ref, hh_ref, ll_ref)


def keep_kernel(lt0, lt1, rt0, rt1, hh_ref, ll_ref, out_ref):
    zh = lax.rem(lax.axis_index("mirror") // NC, NZH)
    blocks(zh, (lt0, lt1), (rt0, rt1), out_ref, hh_ref, ll_ref)


def per_device(colloc, coeffs, targets, pair_list):
    naux, nb = targets.shape[1], targets.shape[2]
    shape = jax.ShapeDtypeStruct
    mates = [(m, m ^ 1) for m in range(MIRROR)]
    mate = lax.ppermute(pair_list, "mirror", mates)
    work = lax.ppermute(targets, "mirror", swap_pairs())[0]
    rows = pl.pallas_call(
        pick_kernel,
        out_shape=shape((colloc.shape[0] // 2, 2 * nb), f32),
        in_specs=[SMEM, SMEM, ANY],
        out_specs=VMEM,
        scratch_shapes=[pltpu.SemaphoreType.DMA((2,))],
        compiler_params=params(8),
        name="pick",
    )(pair_list, mate, colloc)

    z_groups = [[x * NZ + z for z in range(NZ)] for x in range(NX)]
    own = lax.all_gather(rows, "blk", axis=0, tiled=True, axis_index_groups=z_groups)
    h = own.shape[0] // 2
    side0 = lax.ppermute(own[:h], "blk", x_trade(3))
    near1 = lax.ppermute(own[h:], "blk", x_trade(1))
    side1 = lax.ppermute(own[h:], "blk", x_trade(3))
    near0 = lax.ppermute(own[:h], "blk", x_trade(1))
    far1 = lax.ppermute(near1, "blk", x_trade(3))
    far0 = lax.ppermute(side0, "blk", x_trade(1))

    unit = 2 * 1024 * 2048 * 128
    weights = [pltpu.VMEM((naux * nb, 512), bf16)] * 2
    acc, lt0, rt0 = pl.pallas_call(
        fit_first_kernel,
        out_shape=(shape((naux * nb, 2 * nb), f32), shape((nb, 1536), f32), shape((2 * nb, 1536), bf16)),
        in_specs=[VMEM] * 6,
        out_specs=[VMEM] * 3,
        scratch_shapes=weights,
        compiler_params=params(16),
        cost_estimate=cost(3 * unit, 5),
        name="fit_first",
    )(own, near0, near1, side0, side1, coeffs)
    u, lt1, rt1 = pl.pallas_call(
        fit_last_kernel,
        out_shape=(shape((naux, nb, nb), f32), shape((nb, 512), f32), shape((2 * nb, 512), bf16)),
        in_specs=[VMEM] * 5,
        out_specs=[VMEM] * 3,
        scratch_shapes=weights,
        compiler_params=params(16),
        cost_estimate=cost(unit, 3),
        name="fit_last",
    )(far0, far1, acc, coeffs, work)

    other = lax.ppermute(u, "mirror", mates)
    half = shape((NY, naux, nb), f32)
    stacked = shape((naux * nb, 2 * nb), bf16)
    send, hh, ll, res = pl.pallas_call(
        send_kernel,
        out_shape=(half, stacked, stacked, shape((naux, nb, nb), f32)),
        in_specs=[VMEM] * 6,
        out_specs=[VMEM] * 4,
        compiler_params=params(16),
        cost_estimate=cost(2 * unit, 4),
        name="gradient_send",
    )(u, other, lt0, lt1, rt0, rt1)
    residual = lax.ppermute(res[None], "mirror", swap_pairs())
    moved = lax.ppermute(send, "mirror", [(m, m ^ NC) for m in range(MIRROR)])
    keep = pl.pallas_call(
        keep_kernel,
        out_shape=half,
        in_specs=[VMEM] * 6,
        out_specs=VMEM,
        compiler_params=params(16),
        cost_estimate=cost(2 * unit, 4),
        name="gradient_keep",
    )(lt0, lt1, rt0, rt1, hh, ll)
    y_groups = [[(y * NZH + h) * NC + c for y in range(NY)] for h in range(NZH) for c in range(NC)]
    spread = lax.all_to_all(keep + moved, "mirror", 0, 0, tiled=True, axis_index_groups=y_groups)
    return residual, jnp.sum(spread, axis=0)


def solution(mesh):
    return jax.shard_map(
        per_device,
        mesh=mesh,
        in_specs=(
            P("blk", None),
            P("blk", None),
            P("mirror", "blk", None, None),
            P("mirror", None),
        ),
        out_specs=(P("mirror", "blk", None, None), P("blk", "mirror")),
        check_vma=False,
    )
```

```python
import jax
import jax.numpy as jnp
from jax import lax
from jax.experimental import pallas as pl
from jax.experimental.pallas import tpu as pltpu
from jax.sharding import PartitionSpec as P

NX, NZ = 4, 4
NY, NZH, NC = 8, 2, 2
MIRROR = NY * NZH * NC
HALF = MIRROR // 2
bf16, f32 = jnp.bfloat16, jnp.float32
VMEM = pl.BlockSpec(memory_space=pltpu.VMEM)
SMEM = pl.BlockSpec(memory_space=pltpu.SMEM)


def params(mib):
    return pltpu.CompilerParams(vmem_limit_bytes=mib * 1024 * 1024)


def cost(flops, mib):
    return pl.CostEstimate(flops=flops, bytes_accessed=mib << 20, transcendentals=0)


def swap_pairs():
    out = []
    for m in range(MIRROR):
        low = m < HALF
        if low and m % 2 == 1:
            out.append((m, m + HALF - 1))
        elif not low and m % 2 == 0:
            out.append((m, m - HALF + 1))
        else:
            out.append((m, m))
    return out


def x_trade(mask):
    return [(x * NZ + z, (x ^ mask) * NZ + z) for x in range(NX) for z in range(NZ)]


def z_trade(mask):
    return [(x * NZ + z, x * NZ + (z ^ mask)) for x in range(NX) for z in range(NZ)]


def z_order(z):
    near = z + 1 - 2 * lax.rem(z, 2)
    return [z, near, lax.rem(z + 2, NZ), lax.rem(near + 2, NZ)]


def sources(x):
    return [x, x + 1 - 2 * lax.rem(x, 2), NX - 1 - x, lax.rem(x + 2, NX)]


def split(v):
    hi = v.astype(bf16)
    return hi, (v - hi.astype(f32)).astype(bf16)


def pick_kernel(mine_ref, mate_ref, half_ref, out_ref):
    m = lax.axis_index("mirror")
    keeps = lax.rem(m, 2) != (m < HALF).astype(jnp.int32)
    q = jnp.where(keeps, mine_ref[0, 0], mate_ref[0, 0])
    p = jnp.where(keeps, mine_ref[0, 1], mate_ref[0, 1])
    for k, block in enumerate((p, q)):
        out_ref[:, k * 128 : (k + 1) * 128] = half_ref[:, pl.ds(pl.multiple_of(block * 128, 128), 128)]


def fit_part(coef_ref, rows, xs, lt_ref, rt_ref, n, whi, wlo):
    core = lax.rem(lax.axis_index("mirror"), 2)
    left, right = rows[:, :128], rows[:, 128:]
    lt, rt = left.T, right.T
    cols = pl.ds(n * 512, 512)
    lt_ref[:, cols] = lt
    rhi, rlo = split(right)
    rthi, rtlo = split(rt)
    rt_ref[0:128, cols] = rthi
    rt_ref[128:256, cols] = rtlo
    both = jnp.concatenate([rhi, rlo], axis=1)
    cs = []
    for z in z_order(lax.rem(lax.axis_index("blk"), NZ)):
        at = pl.multiple_of((xs * NZ + z) * 256 + core * 128, 128)
        cs.append(coef_ref[:, pl.ds(at, 128)])
    cf = jnp.concatenate(cs, axis=1)
    for a in range(coef_ref.shape[0]):
        hi, lo = split(cf[a : a + 1, :] * lt)
        whi[pl.ds(a * 128, 128), :] = hi
        wlo[pl.ds(a * 128, 128), :] = lo
    part = jnp.dot(whi[...], both, preferred_element_type=f32)
    return part + jnp.dot(wlo[...], both, preferred_element_type=f32)


def fit_first_kernel(own0, own1, own2, own3, near0, near1, side0, side1, coef_ref, acc_ref, lt_ref, rt_ref, whi, wlo):
    xs = sources(lax.axis_index("blk") // NZ)
    for n, refs in enumerate(((own0, own1, own2, own3), (near0, near1), (side0, side1))):
        rows = jnp.concatenate([r[...] for r in refs], axis=0)
        part = fit_part(coef_ref, rows, xs[n], lt_ref, rt_ref, n, whi, wlo)
        if n == 0:
            acc_ref[...] = part
        else:
            acc_ref[...] += part


def fit_last_kernel(far0, far1, acc_ref, coef_ref, t_ref, u_ref, lt_ref, rt_ref, whi, wlo):
    xs = sources(lax.axis_index("blk") // NZ)
    rows = jnp.concatenate([far0[...], far1[...]], axis=0)
    tot = acc_ref[...] + fit_part(coef_ref, rows, xs[3], lt_ref, rt_ref, 0, whi, wlo)
    fit = tot[:, :128] + tot[:, 128:]
    u_ref[...] = 0.5 * t_ref[...] - fit.reshape(t_ref.shape)


def blocks(parity, lt_refs, rt_refs, out_ref, hh, ll):
    z = lax.rem(lax.axis_index("blk"), NZ)
    first, pair = lax.rem(z + parity, 2), z // 2
    for n, xs in enumerate(sources(lax.axis_index("blk") // NZ)):
        lt_ref, rt_ref = (lt_refs[0], rt_refs[0]) if n < 3 else (lt_refs[1], rt_refs[1])
        at = n * 512 if n < 3 else 0
        cols = [pl.ds(pl.multiple_of(at + j * 256 + first * 128, 128), 128) for j in range(2)]
        rt = jnp.concatenate([rt_ref[:, c] for c in cols], axis=1)
        lt = jnp.concatenate([lt_ref[:, c] for c in cols], axis=1)
        spread = jnp.dot(hh[...], rt, preferred_element_type=f32)
        spread += jnp.dot(ll[...], rt, preferred_element_type=f32)
        terms = []
        for a in range(out_ref.shape[1]):
            terms.append(jnp.sum(spread[a * 128 : (a + 1) * 128] * lt, axis=0, keepdims=True))
        block = jnp.concatenate(terms, axis=0)
        for j in range(2):
            out_ref[xs * 2 + (pair if j == 0 else 1 - pair)] = block[:, j * 128 : (j + 1) * 128]


def send_kernel(u_ref, o_ref, lt0, lt1, rt0, rt1, out_ref, hh_ref, ll_ref, r_ref):
    zh = lax.rem(lax.axis_index("mirror") // NC, NZH)
    for a in range(u_ref.shape[0]):
        r = u_ref[a] + o_ref[a].T
        r_ref[a] = r
        hi, lo = split(2.0 * r)
        rows = pl.ds(a * 128, 128)
        hh_ref[rows, 0:128] = hi
        hh_ref[rows, 128:256] = hi
        ll_ref[rows, 0:128] = lo
        ll_ref[rows, 128:256] = lo
    blocks(1 - zh, (lt0, lt1), (rt0, rt1), out_ref, hh_ref, ll_ref)


def keep_kernel(lt0, lt1, rt0, rt1, hh_ref, ll_ref, out_ref):
    zh = lax.rem(lax.axis_index("mirror") // NC, NZH)
    blocks(zh, (lt0, lt1), (rt0, rt1), out_ref, hh_ref, ll_ref)


def per_device(colloc, coeffs, targets, pair_list):
    naux, nb = targets.shape[1], targets.shape[2]
    shape = jax.ShapeDtypeStruct
    mates = [(m, m ^ 1) for m in range(MIRROR)]
    mate = lax.ppermute(pair_list, "mirror", mates)
    work = lax.ppermute(targets, "mirror", swap_pairs())[0]
    n = colloc.shape[0] // 2
    core = lax.rem(lax.axis_index("mirror"), 2)
    half = lax.dynamic_slice(colloc, (core * n, 0), (n, colloc.shape[1]))
    rows = pl.pallas_call(
        pick_kernel,
        out_shape=shape((n, 2 * nb), f32),
        in_specs=[SMEM, SMEM, VMEM],
        out_specs=VMEM,
        compiler_params=params(8),
        name="pick",
    )(pair_list[:, ::-1], mate, half)

    z1 = lax.ppermute(rows, "blk", z_trade(1))
    z3 = lax.ppermute(rows, "blk", z_trade(3))
    z2 = lax.ppermute(rows, "blk", z_trade(2))
    early = jnp.concatenate([rows, z1], axis=0)
    late = jnp.concatenate([z2, z3], axis=0)
    side0 = lax.ppermute(early, "blk", x_trade(3))
    near0 = lax.ppermute(early, "blk", x_trade(1))
    near1 = lax.ppermute(late, "blk", x_trade(1))
    side1 = lax.ppermute(late, "blk", x_trade(3))
    far0 = lax.ppermute(side0, "blk", x_trade(1))
    far1 = lax.ppermute(near1, "blk", x_trade(3))

    unit = 2 * 1024 * 2048 * 128
    weights = [pltpu.VMEM((naux * nb, 512), bf16)] * 2
    acc, lt0, rt0 = pl.pallas_call(
        fit_first_kernel,
        out_shape=(shape((naux * nb, 2 * nb), f32), shape((nb, 1536), f32), shape((2 * nb, 1536), bf16)),
        in_specs=[VMEM] * 9,
        out_specs=[VMEM] * 3,
        scratch_shapes=weights,
        compiler_params=params(16),
        cost_estimate=cost(3 * unit, 5),
        name="fit_first",
    )(rows, z1, z2, z3, near0, near1, side0, side1, coeffs)
    u, lt1, rt1 = pl.pallas_call(
        fit_last_kernel,
        out_shape=(shape((naux, nb, nb), f32), shape((nb, 512), f32), shape((2 * nb, 512), bf16)),
        in_specs=[VMEM] * 5,
        out_specs=[VMEM] * 3,
        scratch_shapes=weights,
        compiler_params=params(16),
        cost_estimate=cost(unit, 3),
        name="fit_last",
    )(far0, far1, acc, coeffs, work)

    other = lax.ppermute(u, "mirror", mates)
    eight = shape((NY, naux, nb), f32)
    stacked = shape((naux * nb, 2 * nb), bf16)
    send, hh, ll, res = pl.pallas_call(
        send_kernel,
        out_shape=(eight, stacked, stacked, shape((naux, nb, nb), f32)),
        in_specs=[VMEM] * 6,
        out_specs=[VMEM] * 4,
        compiler_params=params(16),
        cost_estimate=cost(2 * unit, 4),
        name="gradient_send",
    )(u, other, lt0, lt1, rt0, rt1)
    residual = lax.ppermute(res[None], "mirror", swap_pairs())
    moved = lax.ppermute(send, "mirror", [(m, m ^ NC) for m in range(MIRROR)])
    keep = pl.pallas_call(
        keep_kernel,
        out_shape=eight,
        in_specs=[VMEM] * 6,
        out_specs=VMEM,
        compiler_params=params(16),
        cost_estimate=cost(2 * unit, 4),
        name="gradient_keep",
    )(lt0, lt1, rt0, rt1, hh, ll)
    y_groups = [[(y * NZH + h) * NC + c for y in range(NY)] for h in range(NZH) for c in range(NC)]
    spread = lax.all_to_all(keep + moved, "mirror", 0, 0, tiled=True, axis_index_groups=y_groups)
    return residual, jnp.sum(spread, axis=0)


def solution(mesh):
    return jax.shard_map(
        per_device,
        mesh=mesh,
        in_specs=(
            P("blk", None),
            P("blk", None),
            P("mirror", "blk", None, None),
            P("mirror", None),
        ),
        out_specs=(P("mirror", "blk", None, None), P("blk", "mirror")),
        check_vma=False,
    )
```

```python
import jax
import jax.numpy as jnp
from jax import lax
from jax.experimental import pallas as pl
from jax.experimental.pallas import tpu as pltpu
from jax.sharding import PartitionSpec as P

NX, NZ = 4, 4
NY, NZH, NC = 8, 2, 2
MIRROR = NY * NZH * NC
HALF = MIRROR // 2
bf16, f32 = jnp.bfloat16, jnp.float32
VMEM = pl.BlockSpec(memory_space=pltpu.VMEM)
SMEM = pl.BlockSpec(memory_space=pltpu.SMEM)


def params(mib):
    return pltpu.CompilerParams(vmem_limit_bytes=mib * 1024 * 1024)


def cost(flops, mib):
    return pl.CostEstimate(flops=flops, bytes_accessed=mib << 20, transcendentals=0)


def swap_pairs():
    out = []
    for m in range(MIRROR):
        low = m < HALF
        if low and m % 2 == 1:
            out.append((m, m + HALF - 1))
        elif not low and m % 2 == 0:
            out.append((m, m - HALF + 1))
        else:
            out.append((m, m))
    return out


def x_trade(mask):
    return [(x * NZ + z, (x ^ mask) * NZ + z) for x in range(NX) for z in range(NZ)]


def z_trade(mask):
    return [(x * NZ + z, x * NZ + (z ^ mask)) for x in range(NX) for z in range(NZ)]


def z_order(z):
    near = z + 1 - 2 * lax.rem(z, 2)
    return [z, near, lax.rem(z + 2, NZ), lax.rem(near + 2, NZ)]


def sources(x):
    return [x, x + 1 - 2 * lax.rem(x, 2), NX - 1 - x, lax.rem(x + 2, NX)]


def split(v):
    hi = v.astype(bf16)
    return hi, (v - hi.astype(f32)).astype(bf16)


def pick_kernel(mine_ref, mate_ref, half_ref, out_ref):
    m = lax.axis_index("mirror")
    keeps = lax.rem(m, 2) != (m < HALF).astype(jnp.int32)
    q = jnp.where(keeps, mine_ref[0, 0], mate_ref[0, 0])
    p = jnp.where(keeps, mine_ref[0, 1], mate_ref[0, 1])
    for k, block in enumerate((p, q)):
        out_ref[:, k * 128 : (k + 1) * 128] = half_ref[:, pl.ds(pl.multiple_of(block * 128, 128), 128)]


def fit_part(coef_ref, rows, xs, zs, lt_ref, rt_ref, at, whi, wlo):
    core = lax.rem(lax.axis_index("mirror"), 2)
    left, right = rows[:, :128], rows[:, 128:]
    lt, rt = left.T, right.T
    wide = rows.shape[0]
    cols = pl.ds(at, wide)
    lt_ref[:, cols] = lt
    rhi, rlo = split(right)
    rthi, rtlo = split(rt)
    rt_ref[0:128, cols] = rthi
    rt_ref[128:256, cols] = rtlo
    both = jnp.concatenate([rhi, rlo], axis=1)
    cs = []
    for z in zs:
        start = pl.multiple_of((xs * NZ + z) * 256 + core * 128, 128)
        cs.append(coef_ref[:, pl.ds(start, 128)])
    cf = jnp.concatenate(cs, axis=1)
    for a in range(coef_ref.shape[0]):
        hi, lo = split(cf[a : a + 1, :] * lt)
        whi[pl.ds(a * 128, 128), 0:wide] = hi
        wlo[pl.ds(a * 128, 128), 0:wide] = lo
    part = jnp.dot(whi[:, 0:wide], both, preferred_element_type=f32)
    return part + jnp.dot(wlo[:, 0:wide], both, preferred_element_type=f32)


def fit_first_kernel(own0, own1, own2, own3, near0, near1, side0, side1, coef_ref, acc_ref, lt_ref, rt_ref, whi, wlo):
    xs = sources(lax.axis_index("blk") // NZ)
    zs = z_order(lax.rem(lax.axis_index("blk"), NZ))
    for n, refs in enumerate(((own0, own1, own2, own3), (near0, near1), (side0, side1))):
        rows = jnp.concatenate([r[...] for r in refs], axis=0)
        part = fit_part(coef_ref, rows, xs[n], zs, lt_ref, rt_ref, n * 512, whi, wlo)
        if n == 0:
            acc_ref[...] = part
        else:
            acc_ref[...] += part


def fit_next_kernel(far0, acc_ref, coef_ref, out_ref, lt_ref, rt_ref, whi, wlo):
    xs = sources(lax.axis_index("blk") // NZ)
    zs = z_order(lax.rem(lax.axis_index("blk"), NZ))
    out_ref[...] = acc_ref[...] + fit_part(coef_ref, far0[...], xs[3], zs[:2], lt_ref, rt_ref, 0, whi, wlo)


def fit_last_kernel(far1, acc_ref, coef_ref, t_ref, u_ref, lt_ref, rt_ref, whi, wlo):
    xs = sources(lax.axis_index("blk") // NZ)
    zs = z_order(lax.rem(lax.axis_index("blk"), NZ))
    tot = acc_ref[...] + fit_part(coef_ref, far1[...], xs[3], zs[2:], lt_ref, rt_ref, 0, whi, wlo)
    fit = tot[:, :128] + tot[:, 128:]
    u_ref[...] = 0.5 * t_ref[...] - fit.reshape(t_ref.shape)


def blocks(parity, lt_refs, rt_refs, out_ref, hh, ll):
    z = lax.rem(lax.axis_index("blk"), NZ)
    first, pair = lax.rem(z + parity, 2), z // 2
    for n, xs in enumerate(sources(lax.axis_index("blk") // NZ)):
        places = [(0, n * 512 + j * 256) for j in range(2)] if n < 3 else [(1, 0), (2, 0)]
        cols = [(i, pl.ds(pl.multiple_of(at + first * 128, 128), 128)) for i, at in places]
        rt = jnp.concatenate([rt_refs[i][:, c] for i, c in cols], axis=1)
        lt = jnp.concatenate([lt_refs[i][:, c] for i, c in cols], axis=1)
        spread = jnp.dot(hh[...], rt, preferred_element_type=f32)
        spread += jnp.dot(ll[...], rt, preferred_element_type=f32)
        terms = []
        for a in range(out_ref.shape[1]):
            terms.append(jnp.sum(spread[a * 128 : (a + 1) * 128] * lt, axis=0, keepdims=True))
        block = jnp.concatenate(terms, axis=0)
        for j in range(2):
            out_ref[xs * 2 + (pair if j == 0 else 1 - pair)] = block[:, j * 128 : (j + 1) * 128]


def send_kernel(u_ref, o_ref, lt0, lt1, lt2, rt0, rt1, rt2, out_ref, hh_ref, ll_ref, r_ref):
    zh = lax.rem(lax.axis_index("mirror") // NC, NZH)
    for a in range(u_ref.shape[0]):
        r = u_ref[a] + o_ref[a].T
        r_ref[a] = r
        hi, lo = split(2.0 * r)
        rows = pl.ds(a * 128, 128)
        hh_ref[rows, 0:128] = hi
        hh_ref[rows, 128:256] = hi
        ll_ref[rows, 0:128] = lo
        ll_ref[rows, 128:256] = lo
    blocks(1 - zh, (lt0, lt1, lt2), (rt0, rt1, rt2), out_ref, hh_ref, ll_ref)


def keep_kernel(lt0, lt1, lt2, rt0, rt1, rt2, hh_ref, ll_ref, out_ref):
    zh = lax.rem(lax.axis_index("mirror") // NC, NZH)
    blocks(zh, (lt0, lt1, lt2), (rt0, rt1, rt2), out_ref, hh_ref, ll_ref)


def per_device(colloc, coeffs, targets, pair_list):
    naux, nb = targets.shape[1], targets.shape[2]
    shape = jax.ShapeDtypeStruct
    mates = [(m, m ^ 1) for m in range(MIRROR)]
    mate = lax.ppermute(pair_list, "mirror", mates)
    work = lax.ppermute(targets, "mirror", swap_pairs())[0]
    n = colloc.shape[0] // 2
    core = lax.rem(lax.axis_index("mirror"), 2)
    half = lax.dynamic_slice(colloc, (core * n, 0), (n, colloc.shape[1]))
    rows = pl.pallas_call(
        pick_kernel,
        out_shape=shape((n, 2 * nb), f32),
        in_specs=[SMEM, SMEM, VMEM],
        out_specs=VMEM,
        compiler_params=params(8),
        name="pick",
    )(pair_list[:, ::-1], mate, half)

    z1 = lax.ppermute(rows, "blk", z_trade(1))
    z3 = lax.ppermute(rows, "blk", z_trade(3))
    z2 = lax.ppermute(rows, "blk", z_trade(2))
    early = jnp.concatenate([rows, z1], axis=0)
    late = jnp.concatenate([z2, z3], axis=0)
    side0 = lax.ppermute(early, "blk", x_trade(3))
    near0 = lax.ppermute(early, "blk", x_trade(1))
    near1 = lax.ppermute(late, "blk", x_trade(1))
    side1 = lax.ppermute(late, "blk", x_trade(3))
    far0 = lax.ppermute(side0, "blk", x_trade(1))
    far1 = lax.ppermute(near1, "blk", x_trade(3))

    unit = 2 * 1024 * 2048 * 128
    weights = [pltpu.VMEM((naux * nb, 512), bf16)] * 2
    acc, lt0, rt0 = pl.pallas_call(
        fit_first_kernel,
        out_shape=(shape((naux * nb, 2 * nb), f32), shape((nb, 1536), f32), shape((2 * nb, 1536), bf16)),
        in_specs=[VMEM] * 9,
        out_specs=[VMEM] * 3,
        scratch_shapes=weights,
        compiler_params=params(16),
        cost_estimate=cost(3 * unit, 5),
        name="fit_first",
    )(rows, z1, z2, z3, near0, near1, side0, side1, coeffs)
    acc, lt1, rt1 = pl.pallas_call(
        fit_next_kernel,
        out_shape=(shape((naux * nb, 2 * nb), f32), shape((nb, 256), f32), shape((2 * nb, 256), bf16)),
        in_specs=[VMEM] * 3,
        out_specs=[VMEM] * 3,
        scratch_shapes=weights,
        compiler_params=params(16),
        cost_estimate=cost(unit // 2, 3),
        name="fit_next",
    )(far0, acc, coeffs)
    u, lt2, rt2 = pl.pallas_call(
        fit_last_kernel,
        out_shape=(shape((naux, nb, nb), f32), shape((nb, 256), f32), shape((2 * nb, 256), bf16)),
        in_specs=[VMEM] * 4,
        out_specs=[VMEM] * 3,
        scratch_shapes=weights,
        compiler_params=params(16),
        cost_estimate=cost(unit // 2, 3),
        name="fit_last",
    )(far1, acc, coeffs, work)

    other = lax.ppermute(u, "mirror", mates)
    eight = shape((NY, naux, nb), f32)
    stacked = shape((naux * nb, 2 * nb), bf16)
    send, hh, ll, res = pl.pallas_call(
        send_kernel,
        out_shape=(eight, stacked, stacked, shape((naux, nb, nb), f32)),
        in_specs=[VMEM] * 8,
        out_specs=[VMEM] * 4,
        compiler_params=params(16),
        cost_estimate=cost(2 * unit, 4),
        name="gradient_send",
    )(u, other, lt0, lt1, lt2, rt0, rt1, rt2)
    residual = lax.ppermute(res[None], "mirror", swap_pairs())
    moved = lax.ppermute(send, "mirror", [(m, m ^ NC) for m in range(MIRROR)])
    keep = pl.pallas_call(
        keep_kernel,
        out_shape=eight,
        in_specs=[VMEM] * 8,
        out_specs=VMEM,
        compiler_params=params(16),
        cost_estimate=cost(2 * unit, 4),
        name="gradient_keep",
    )(lt0, lt1, lt2, rt0, rt1, rt2, hh, ll)
    y_groups = [[(y * NZH + h) * NC + c for y in range(NY)] for h in range(NZH) for c in range(NC)]
    spread = lax.all_to_all(keep + moved, "mirror", 0, 0, tiled=True, axis_index_groups=y_groups)
    return residual, jnp.sum(spread, axis=0)


def solution(mesh):
    return jax.shard_map(
        per_device,
        mesh=mesh,
        in_specs=(
            P("blk", None),
            P("blk", None),
            P("mirror", "blk", None, None),
            P("mirror", None),
        ),
        out_specs=(P("mirror", "blk", None, None), P("blk", "mirror")),
        check_vma=False,
    )
```

```python
import jax
import jax.numpy as jnp
from jax import lax
from jax.experimental import pallas as pl
from jax.experimental.pallas import tpu as pltpu
from jax.sharding import PartitionSpec as P

NX, NZ = 4, 4
NY, NZH, NC = 8, 2, 2
MIRROR = NY * NZH * NC
HALF = MIRROR // 2
bf16, f32 = jnp.bfloat16, jnp.float32
VMEM = pl.BlockSpec(memory_space=pltpu.VMEM)
SMEM = pl.BlockSpec(memory_space=pltpu.SMEM)


def params(mib):
    return pltpu.CompilerParams(vmem_limit_bytes=mib * 1024 * 1024)


def cost(flops, mib):
    return pl.CostEstimate(flops=flops, bytes_accessed=mib << 20, transcendentals=0)


def swap_pairs():
    out = []
    for m in range(MIRROR):
        low = m < HALF
        if low and m % 2 == 1:
            out.append((m, m + HALF - 1))
        elif not low and m % 2 == 0:
            out.append((m, m - HALF + 1))
        else:
            out.append((m, m))
    return out


def x_trade(mask):
    return [(x * NZ + z, (x ^ mask) * NZ + z) for x in range(NX) for z in range(NZ)]


def z_trade(mask):
    return [(x * NZ + z, x * NZ + (z ^ mask)) for x in range(NX) for z in range(NZ)]


def z_order(z):
    near = z + 1 - 2 * lax.rem(z, 2)
    return [z, near, lax.rem(z + 2, NZ), lax.rem(near + 2, NZ)]


def sources(x):
    return [x, x + 1 - 2 * lax.rem(x, 2), NX - 1 - x, lax.rem(x + 2, NX)]


def split(v):
    hi = v.astype(bf16)
    return hi, (v - hi.astype(f32)).astype(bf16)


def pick_kernel(mine_ref, mate_ref, half_ref, out_ref):
    m = lax.axis_index("mirror")
    keeps = lax.rem(m, 2) != (m < HALF).astype(jnp.int32)
    q = jnp.where(keeps, mine_ref[0, 0], mate_ref[0, 0])
    p = jnp.where(keeps, mine_ref[0, 1], mate_ref[0, 1])
    for k, block in enumerate((p, q)):
        out_ref[:, k * 128 : (k + 1) * 128] = half_ref[:, pl.ds(pl.multiple_of(block * 128, 128), 128)]


def fit_part(coef_ref, rows, xs, zs, lt_ref, rt_ref, at, whi, wlo):
    core = lax.rem(lax.axis_index("mirror"), 2)
    left, right = rows[:, :128], rows[:, 128:]
    lt, rt = left.T, right.T
    wide = rows.shape[0]
    cols = pl.ds(at, wide)
    lt_ref[:, cols] = lt
    rhi, rlo = split(right)
    rthi, rtlo = split(rt)
    rt_ref[0:128, cols] = rthi
    rt_ref[128:256, cols] = rtlo
    both = jnp.concatenate([rhi, rlo], axis=1)
    cs = []
    for z in zs:
        start = pl.multiple_of((xs * NZ + z) * 256 + core * 128, 128)
        cs.append(coef_ref[:, pl.ds(start, 128)])
    cf = jnp.concatenate(cs, axis=1)
    for a in range(coef_ref.shape[0]):
        hi, lo = split(cf[a : a + 1, :] * lt)
        whi[pl.ds(a * 128, 128), 0:wide] = hi
        wlo[pl.ds(a * 128, 128), 0:wide] = lo
    part = jnp.dot(whi[:, 0:wide], both, preferred_element_type=f32)
    return part + jnp.dot(wlo[:, 0:wide], both, preferred_element_type=f32)


def fit_first_kernel(own0, own1, own2, own3, near0, near1, side0, side1, coef_ref, acc_ref, lt_ref, rt_ref, whi, wlo):
    xs = sources(lax.axis_index("blk") // NZ)
    zs = z_order(lax.rem(lax.axis_index("blk"), NZ))
    for n, refs in enumerate(((own0, own1, own2, own3), (near0, near1), (side0, side1))):
        rows = jnp.concatenate([r[...] for r in refs], axis=0)
        part = fit_part(coef_ref, rows, xs[n], zs, lt_ref, rt_ref, n * 512, whi, wlo)
        if n == 0:
            acc_ref[...] = part
        else:
            acc_ref[...] += part


def fit_next_kernel(far0, acc_ref, coef_ref, out_ref, lt_ref, rt_ref, whi, wlo):
    xs = sources(lax.axis_index("blk") // NZ)
    zs = z_order(lax.rem(lax.axis_index("blk"), NZ))
    out_ref[...] = acc_ref[...] + fit_part(coef_ref, far0[...], xs[3], zs[:2], lt_ref, rt_ref, 0, whi, wlo)


def fit_last_kernel(far1, acc_ref, coef_ref, t_ref, u_ref, lt_ref, rt_ref, whi, wlo):
    xs = sources(lax.axis_index("blk") // NZ)
    zs = z_order(lax.rem(lax.axis_index("blk"), NZ))
    tot = acc_ref[...] + fit_part(coef_ref, far1[...], xs[3], zs[2:], lt_ref, rt_ref, 0, whi, wlo)
    fit = tot[:, :128] + tot[:, 128:]
    u_ref[...] = 0.5 * t_ref[...] - fit.reshape(t_ref.shape)


def blocks(parity, lt_refs, rt_refs, out_ref, hh, ll):
    z = lax.rem(lax.axis_index("blk"), NZ)
    first, pair = lax.rem(z + parity, 2), z // 2
    for n, xs in enumerate(sources(lax.axis_index("blk") // NZ)):
        places = [(0, n * 512 + j * 256) for j in range(2)] if n < 3 else [(1, 0), (2, 0)]
        cols = [(i, pl.ds(pl.multiple_of(at + first * 128, 128), 128)) for i, at in places]
        rt = jnp.concatenate([rt_refs[i][:, c] for i, c in cols], axis=1)
        lt = jnp.concatenate([lt_refs[i][:, c] for i, c in cols], axis=1)
        spread = jnp.dot(hh[...], rt, preferred_element_type=f32)
        spread += jnp.dot(ll[...], rt, preferred_element_type=f32)
        terms = []
        for a in range(out_ref.shape[1]):
            terms.append(jnp.sum(spread[a * 128 : (a + 1) * 128] * lt, axis=0, keepdims=True))
        block = jnp.concatenate(terms, axis=0)
        for j in range(2):
            out_ref[xs * 2 + (pair if j == 0 else 1 - pair)] = block[:, j * 128 : (j + 1) * 128]


def residual_kernel(u_ref, o_ref, r_ref):
    for a in range(u_ref.shape[0]):
        r_ref[a] = u_ref[a] + o_ref[a].T


def send_kernel(r_ref, lt0, lt1, lt2, rt0, rt1, rt2, out_ref, hh_ref, ll_ref):
    zh = lax.rem(lax.axis_index("mirror") // NC, NZH)
    for a in range(r_ref.shape[0]):
        hi, lo = split(2.0 * r_ref[a])
        rows = pl.ds(a * 128, 128)
        hh_ref[rows, 0:128] = hi
        hh_ref[rows, 128:256] = hi
        ll_ref[rows, 0:128] = lo
        ll_ref[rows, 128:256] = lo
    blocks(1 - zh, (lt0, lt1, lt2), (rt0, rt1, rt2), out_ref, hh_ref, ll_ref)


def keep_kernel(lt0, lt1, lt2, rt0, rt1, rt2, hh_ref, ll_ref, out_ref):
    zh = lax.rem(lax.axis_index("mirror") // NC, NZH)
    blocks(zh, (lt0, lt1, lt2), (rt0, rt1, rt2), out_ref, hh_ref, ll_ref)


def per_device(colloc, coeffs, targets, pair_list):
    naux, nb = targets.shape[1], targets.shape[2]
    shape = jax.ShapeDtypeStruct
    mates = [(m, m ^ 1) for m in range(MIRROR)]
    mate = lax.ppermute(pair_list, "mirror", mates)
    work = lax.ppermute(targets, "mirror", swap_pairs())[0]
    n = colloc.shape[0] // 2
    core = lax.rem(lax.axis_index("mirror"), 2)
    half = lax.dynamic_slice(colloc, (core * n, 0), (n, colloc.shape[1]))
    rows = pl.pallas_call(
        pick_kernel,
        out_shape=shape((n, 2 * nb), f32),
        in_specs=[SMEM, SMEM, VMEM],
        out_specs=VMEM,
        compiler_params=params(8),
        name="pick",
    )(pair_list[:, ::-1], mate, half)

    z1 = lax.ppermute(rows, "blk", z_trade(1))
    z3 = lax.ppermute(rows, "blk", z_trade(3))
    z2 = lax.ppermute(rows, "blk", z_trade(2))
    early = jnp.concatenate([rows, z1], axis=0)
    late = jnp.concatenate([z2, z3], axis=0)
    side0 = lax.ppermute(early, "blk", x_trade(3))
    near0 = lax.ppermute(early, "blk", x_trade(1))
    near1 = lax.ppermute(late, "blk", x_trade(1))
    side1 = lax.ppermute(late, "blk", x_trade(3))
    far0 = lax.ppermute(side0, "blk", x_trade(1))
    far1 = lax.ppermute(near1, "blk", x_trade(3))

    unit = 2 * 1024 * 2048 * 128
    weights = [pltpu.VMEM((naux * nb, 512), bf16)] * 2
    acc, lt0, rt0 = pl.pallas_call(
        fit_first_kernel,
        out_shape=(shape((naux * nb, 2 * nb), f32), shape((nb, 1536), f32), shape((2 * nb, 1536), bf16)),
        in_specs=[VMEM] * 9,
        out_specs=[VMEM] * 3,
        scratch_shapes=weights,
        compiler_params=params(16),
        cost_estimate=cost(3 * unit, 5),
        name="fit_first",
    )(rows, z1, z2, z3, near0, near1, side0, side1, coeffs)
    acc, lt1, rt1 = pl.pallas_call(
        fit_next_kernel,
        out_shape=(shape((naux * nb, 2 * nb), f32), shape((nb, 256), f32), shape((2 * nb, 256), bf16)),
        in_specs=[VMEM] * 3,
        out_specs=[VMEM] * 3,
        scratch_shapes=weights,
        compiler_params=params(16),
        cost_estimate=cost(unit // 2, 3),
        name="fit_next",
    )(far0, acc, coeffs)
    u, lt2, rt2 = pl.pallas_call(
        fit_last_kernel,
        out_shape=(shape((naux, nb, nb), f32), shape((nb, 256), f32), shape((2 * nb, 256), bf16)),
        in_specs=[VMEM] * 4,
        out_specs=[VMEM] * 3,
        scratch_shapes=weights,
        compiler_params=params(16),
        cost_estimate=cost(unit // 2, 3),
        name="fit_last",
    )(far1, acc, coeffs, work)

    other = lax.ppermute(u, "mirror", mates)
    eight = shape((NY, naux, nb), f32)
    stacked = shape((naux * nb, 2 * nb), bf16)
    res = pl.pallas_call(
        residual_kernel,
        out_shape=shape((naux, nb, nb), f32),
        in_specs=[VMEM] * 2,
        out_specs=VMEM,
        compiler_params=params(8),
        cost_estimate=cost(1 << 17, 1),
        name="residual",
    )(u, other)
    send, hh, ll = pl.pallas_call(
        send_kernel,
        out_shape=(eight, stacked, stacked),
        in_specs=[VMEM] * 7,
        out_specs=[VMEM] * 3,
        compiler_params=params(16),
        cost_estimate=cost(2 * unit, 4),
        name="gradient_send",
    )(res, lt0, lt1, lt2, rt0, rt1, rt2)
    residual = lax.ppermute(res[None], "mirror", swap_pairs())
    moved = lax.ppermute(send, "mirror", [(m, m ^ NC) for m in range(MIRROR)])
    keep = pl.pallas_call(
        keep_kernel,
        out_shape=eight,
        in_specs=[VMEM] * 8,
        out_specs=VMEM,
        compiler_params=params(16),
        cost_estimate=cost(2 * unit, 4),
        name="gradient_keep",
    )(lt0, lt1, lt2, rt0, rt1, rt2, hh, ll)
    y_groups = [[(y * NZH + h) * NC + c for y in range(NY)] for h in range(NZH) for c in range(NC)]
    spread = lax.all_to_all(keep + moved, "mirror", 0, 0, tiled=True, axis_index_groups=y_groups)
    return residual, jnp.sum(spread, axis=0)


def solution(mesh):
    return jax.shard_map(
        per_device,
        mesh=mesh,
        in_specs=(
            P("blk", None),
            P("blk", None),
            P("mirror", "blk", None, None),
            P("mirror", None),
        ),
        out_specs=(P("mirror", "blk", None, None), P("blk", "mirror")),
        check_vma=False,
    )
```

```python
import jax
import jax.numpy as jnp
from jax import lax
from jax.experimental import pallas as pl
from jax.experimental.pallas import tpu as pltpu
from jax.sharding import PartitionSpec as P

NX, NZ = 4, 4
NY, NZH, NC = 8, 2, 2
MIRROR = NY * NZH * NC
HALF = MIRROR // 2
bf16, f32 = jnp.bfloat16, jnp.float32
VMEM = pl.BlockSpec(memory_space=pltpu.VMEM)
ANY = pl.BlockSpec(memory_space=pl.ANY)
SMEM = pl.BlockSpec(memory_space=pltpu.SMEM)


def params(mib):
    return pltpu.CompilerParams(vmem_limit_bytes=mib * 1024 * 1024)


def cost(flops, mib):
    return pl.CostEstimate(flops=flops, bytes_accessed=mib << 20, transcendentals=0)


def swap_pairs():
    out = []
    for m in range(MIRROR):
        low = m < HALF
        if low and m % 2 == 1:
            out.append((m, m + HALF - 1))
        elif not low and m % 2 == 0:
            out.append((m, m - HALF + 1))
        else:
            out.append((m, m))
    return out


def x_trade(mask):
    return [(x * NZ + z, (x ^ mask) * NZ + z) for x in range(NX) for z in range(NZ)]


def z_trade(mask):
    return [(x * NZ + z, x * NZ + (z ^ mask)) for x in range(NX) for z in range(NZ)]


def z_order(z):
    near = z + 1 - 2 * lax.rem(z, 2)
    return [z, near, lax.rem(z + 2, NZ), lax.rem(near + 2, NZ)]


def sources(x):
    return [x, x + 1 - 2 * lax.rem(x, 2), NX - 1 - x, lax.rem(x + 2, NX)]


def split(v):
    hi = v.astype(bf16)
    return hi, (v - hi.astype(f32)).astype(bf16)


def pick_kernel(mine_ref, mate_ref, half_ref, out_ref):
    m = lax.axis_index("mirror")
    keeps = lax.rem(m, 2) != (m < HALF).astype(jnp.int32)
    q = jnp.where(keeps, mine_ref[0, 0], mate_ref[0, 0])
    p = jnp.where(keeps, mine_ref[0, 1], mate_ref[0, 1])
    for k, block in enumerate((p, q)):
        out_ref[:, k * 128 : (k + 1) * 128] = half_ref[:, pl.ds(pl.multiple_of(block * 128, 128), 128)]


def fit_part(coef_ref, rows, xs, zs, lt_ref, rt_ref, at, whi, wlo):
    core = lax.rem(lax.axis_index("mirror"), 2)
    left, right = rows[:, :128], rows[:, 128:]
    lt, rt = left.T, right.T
    wide = rows.shape[0]
    cols = pl.ds(at, wide)
    lt_ref[:, cols] = lt
    rhi, rlo = split(right)
    rthi, rtlo = split(rt)
    rt_ref[0:128, cols] = rthi
    rt_ref[128:256, cols] = rtlo
    both = jnp.concatenate([rhi, rlo], axis=1)
    cs = []
    for z in zs:
        start = pl.multiple_of((xs * NZ + z) * 256 + core * 128, 128)
        cs.append(coef_ref[:, pl.ds(start, 128)])
    cf = jnp.concatenate(cs, axis=1)
    for a in range(coef_ref.shape[0]):
        hi, lo = split(cf[a : a + 1, :] * lt)
        whi[pl.ds(a * 128, 128), 0:wide] = hi
        wlo[pl.ds(a * 128, 128), 0:wide] = lo
    part = jnp.dot(whi[:, 0:wide], both, preferred_element_type=f32)
    return part + jnp.dot(wlo[:, 0:wide], both, preferred_element_type=f32)


def fit_first_kernel(own0, own1, own2, own3, near0, near1, side0, side1, coef_ref, acc_ref, lt_ref, rt_ref, whi, wlo):
    xs = sources(lax.axis_index("blk") // NZ)
    zs = z_order(lax.rem(lax.axis_index("blk"), NZ))
    for n, refs in enumerate(((own0, own1, own2, own3), (near0, near1), (side0, side1))):
        rows = jnp.concatenate([r[...] for r in refs], axis=0)
        part = fit_part(coef_ref, rows, xs[n], zs, lt_ref, rt_ref, n * 512, whi, wlo)
        if n == 0:
            acc_ref[...] = part
        else:
            acc_ref[...] += part


def fit_next_kernel(far0, acc_ref, coef_ref, out_ref, lt_ref, rt_ref, whi, wlo):
    xs = sources(lax.axis_index("blk") // NZ)
    zs = z_order(lax.rem(lax.axis_index("blk"), NZ))
    out_ref[...] = acc_ref[...] + fit_part(coef_ref, far0[...], xs[3], zs[:2], lt_ref, rt_ref, 0, whi, wlo)


def fit_last_kernel(far1, acc_ref, coef_ref, t_ref, u_ref, lt_ref, rt_ref, whi, wlo):
    xs = sources(lax.axis_index("blk") // NZ)
    zs = z_order(lax.rem(lax.axis_index("blk"), NZ))
    tot = acc_ref[...] + fit_part(coef_ref, far1[...], xs[3], zs[2:], lt_ref, rt_ref, 0, whi, wlo)
    fit = tot[:, :128] + tot[:, 128:]
    u_ref[...] = 0.5 * t_ref[...] - fit.reshape(t_ref.shape)


def blocks(parity, lt_refs, rt_refs, out_ref, hh, ll):
    z = lax.rem(lax.axis_index("blk"), NZ)
    first, pair = lax.rem(z + parity, 2), z // 2
    for n, xs in enumerate(sources(lax.axis_index("blk") // NZ)):
        places = [(0, n * 512 + j * 256) for j in range(2)] if n < 3 else [(1, 0), (2, 0)]
        cols = [(i, pl.ds(pl.multiple_of(at + first * 128, 128), 128)) for i, at in places]
        rt = jnp.concatenate([rt_refs[i][:, c] for i, c in cols], axis=1)
        lt = jnp.concatenate([lt_refs[i][:, c] for i, c in cols], axis=1)
        spread = jnp.dot(hh[...], rt, preferred_element_type=f32)
        spread += jnp.dot(ll[...], rt, preferred_element_type=f32)
        terms = []
        for a in range(out_ref.shape[1]):
            terms.append(jnp.sum(spread[a * 128 : (a + 1) * 128] * lt, axis=0, keepdims=True))
        block = jnp.concatenate(terms, axis=0)
        for j in range(2):
            out_ref[xs * 2 + (pair if j == 0 else 1 - pair)] = block[:, j * 128 : (j + 1) * 128]


def residual_kernel(u_ref, o_ref, r_ref):
    for a in range(u_ref.shape[0]):
        r_ref[a] = u_ref[a] + o_ref[a].T


def send_kernel(r_ref, lt0, lt1, lt2, rt0, rt1, rt2, out_ref, hh_ref, ll_ref):
    zh = lax.rem(lax.axis_index("mirror") // NC, NZH)
    for a in range(r_ref.shape[0]):
        hi, lo = split(2.0 * r_ref[a])
        rows = pl.ds(a * 128, 128)
        hh_ref[rows, 0:128] = hi
        hh_ref[rows, 128:256] = hi
        ll_ref[rows, 0:128] = lo
        ll_ref[rows, 128:256] = lo
    blocks(1 - zh, (lt0, lt1, lt2), (rt0, rt1, rt2), out_ref, hh_ref, ll_ref)


def keep_kernel(lt0, lt1, lt2, rt0, rt1, rt2, hh_ref, ll_ref, out_ref):
    zh = lax.rem(lax.axis_index("mirror") // NC, NZH)
    blocks(zh, (lt0, lt1, lt2), (rt0, rt1, rt2), out_ref, hh_ref, ll_ref)


def finish_kernel(s_ref, back_ref, out_ref, residual_ref, sem):
    copy = pltpu.make_async_copy(back_ref, residual_ref, sem)
    copy.start()
    out_ref[...] = jnp.sum(s_ref[...], axis=0)
    copy.wait()


def per_device(colloc, coeffs, targets, pair_list):
    naux, nb = targets.shape[1], targets.shape[2]
    shape = jax.ShapeDtypeStruct
    mates = [(m, m ^ 1) for m in range(MIRROR)]
    mate = lax.ppermute(pair_list, "mirror", mates)
    work = lax.ppermute(targets, "mirror", swap_pairs())[0]
    n = colloc.shape[0] // 2
    core = lax.rem(lax.axis_index("mirror"), 2)
    half = lax.dynamic_slice(colloc, (core * n, 0), (n, colloc.shape[1]))
    rows = pl.pallas_call(
        pick_kernel,
        out_shape=shape((n, 2 * nb), f32),
        in_specs=[SMEM, SMEM, VMEM],
        out_specs=VMEM,
        compiler_params=params(8),
        name="pick",
    )(pair_list[:, ::-1], mate, half)

    z1 = lax.ppermute(rows, "blk", z_trade(1))
    z3 = lax.ppermute(rows, "blk", z_trade(3))
    z2 = lax.ppermute(rows, "blk", z_trade(2))
    early = jnp.concatenate([rows, z1], axis=0)
    late = jnp.concatenate([z2, z3], axis=0)
    side0 = lax.ppermute(early, "blk", x_trade(3))
    near0 = lax.ppermute(early, "blk", x_trade(1))
    near1 = lax.ppermute(late, "blk", x_trade(1))
    side1 = lax.ppermute(late, "blk", x_trade(3))
    far0 = lax.ppermute(side0, "blk", x_trade(1))
    far1 = lax.ppermute(near1, "blk", x_trade(3))

    unit = 2 * 1024 * 2048 * 128
    weights = [pltpu.VMEM((naux * nb, 512), bf16)] * 2
    acc, lt0, rt0 = pl.pallas_call(
        fit_first_kernel,
        out_shape=(shape((naux * nb, 2 * nb), f32), shape((nb, 1536), f32), shape((2 * nb, 1536), bf16)),
        in_specs=[VMEM] * 9,
        out_specs=[VMEM] * 3,
        scratch_shapes=weights,
        compiler_params=params(16),
        cost_estimate=cost(3 * unit, 5),
        name="fit_first",
    )(rows, z1, z2, z3, near0, near1, side0, side1, coeffs)
    acc, lt1, rt1 = pl.pallas_call(
        fit_next_kernel,
        out_shape=(shape((naux * nb, 2 * nb), f32), shape((nb, 256), f32), shape((2 * nb, 256), bf16)),
        in_specs=[VMEM] * 3,
        out_specs=[VMEM] * 3,
        scratch_shapes=weights,
        compiler_params=params(16),
        cost_estimate=cost(unit // 2, 3),
        name="fit_next",
    )(far0, acc, coeffs)
    u, lt2, rt2 = pl.pallas_call(
        fit_last_kernel,
        out_shape=(shape((naux, nb, nb), f32), shape((nb, 256), f32), shape((2 * nb, 256), bf16)),
        in_specs=[VMEM] * 4,
        out_specs=[VMEM] * 3,
        scratch_shapes=weights,
        compiler_params=params(16),
        cost_estimate=cost(unit // 2, 3),
        name="fit_last",
    )(far1, acc, coeffs, work)

    other = lax.ppermute(u, "mirror", mates)
    eight = shape((NY, naux, nb), f32)
    stacked = shape((naux * nb, 2 * nb), bf16)
    res = pl.pallas_call(
        residual_kernel,
        out_shape=shape((naux, nb, nb), f32),
        in_specs=[VMEM] * 2,
        out_specs=VMEM,
        compiler_params=params(8),
        cost_estimate=cost(1 << 17, 1),
        name="residual",
    )(u, other)
    send, hh, ll = pl.pallas_call(
        send_kernel,
        out_shape=(eight, stacked, stacked),
        in_specs=[VMEM] * 7,
        out_specs=[VMEM] * 3,
        compiler_params=params(16),
        cost_estimate=cost(2 * unit, 4),
        name="gradient_send",
    )(res, lt0, lt1, lt2, rt0, rt1, rt2)
    residual = lax.ppermute(res[None], "mirror", swap_pairs())
    moved = lax.ppermute(send, "mirror", [(m, m ^ NC) for m in range(MIRROR)])
    keep = pl.pallas_call(
        keep_kernel,
        out_shape=eight,
        in_specs=[VMEM] * 8,
        out_specs=VMEM,
        compiler_params=params(16),
        cost_estimate=cost(2 * unit, 4),
        name="gradient_keep",
    )(lt0, lt1, lt2, rt0, rt1, rt2, hh, ll)
    y_groups = [[(y * NZH + h) * NC + c for y in range(NY)] for h in range(NZH) for c in range(NC)]
    spread = lax.all_to_all(keep + moved, "mirror", 0, 0, tiled=True, axis_index_groups=y_groups)
    gradient, residual = pl.pallas_call(
        finish_kernel,
        out_shape=(shape((naux, nb), f32), shape(residual.shape, f32)),
        in_specs=[VMEM, ANY],
        out_specs=[VMEM, ANY],
        scratch_shapes=[pltpu.SemaphoreType.DMA],
        compiler_params=params(8),
        cost_estimate=cost(1 << 17, 1),
        name="finish",
    )(spread, residual)
    return residual, gradient


def solution(mesh):
    return jax.shard_map(
        per_device,
        mesh=mesh,
        in_specs=(
            P("blk", None),
            P("blk", None),
            P("mirror", "blk", None, None),
            P("mirror", None),
        ),
        out_specs=(P("mirror", "blk", None, None), P("blk", "mirror")),
        check_vma=False,
    )
```
